1024 devices in a mesh: expert: 16 (over y, core), dp: 64 (over z, x).
Axes of the slice: x: 8, y: 8, z: 8, core: 2. Of those that a mesh axis runs over, the one named last changes fastest.
Arguments:
- output_grad: bfloat16 [192, 7168], P('expert', 'dp'), may hold values from -6 to 6
- routing: int32 [192, 8], P('expert'), may hold values from 0 to 47, all different within a row; in each aligned block of 12 rows (0 to 11, 12 to 23, ...) at most 4 rows name the same one
- gates: float32 [192, 8], P('expert'), may hold values from 0.1 to 1
- saved_inputs: bfloat16 [48, 64, 7168], P('expert', None, 'dp'), may hold values from -6 to 6
- gate_up: bfloat16 [48, 7168, 2048], P('expert', 'dp'), may hold values from -0.0625 to 0.0625
- down_weight: bfloat16 [48, 1024, 7168], P('expert', None, 'dp'), may hold values from -0.0625 to 0.0625
Outputs:
- input_grad: bfloat16 [192, 7168], P('expert', 'dp')
- gate_up_grad: bfloat16 [48, 7168, 2048], P('expert', 'dp')
The draws below stay inside these ranges and needn't reach their ends.
Inputs may be any that keep to these rules, and one draw needn't show every extreme that they name: `routing`: each token names 8 different experts. Among the routes of one block of 12 tokens no expert is named more than 4 times, a bound that some block reaches.
All inputs are finite; a program needn't handle non-finite values.
Results may differ from the reference program's by a relative error of at most 0.0064.
Values may be sent and summed in bfloat16 or wider, within the bound.
A program may use at most 32 MiB of HBM per device.

```python
import math
import jax
import jax.numpy as jnp
import numpy as np
from jax import lax

D = 7168
F = 1024
TOPK = 8
TOK_DEV = 12
EXPERTS = 48
CAP = 4
SLOTS = 64
TOKENS = 192
N_EXPERT = 16


def block_scale(key, extent, split, low, largest):
    level, own = 1.0, jax.random.fold_in(key, 6)
    for axis_at, parts in split:
        steps = jnp.exp(jax.random.uniform(jax.random.fold_in(own, axis_at), (parts,), jnp.float32, low / len(split), largest / len(split)))
        level = level * jnp.repeat(steps, extent[axis_at] // parts).reshape([-1 if axis == axis_at else 1 for axis in range(len(extent))])
    return level


def shared_out(stream_key, own, number, rows, amount, top, reach, skew):
    sequence = jax.random.permutation(stream_key, amount)
    crowded, common = load_shares(amount, rows * top, reach, skew, True), load_shares(amount, rows * top, reach, skew, False)
    places = jnp.arange(amount)

    def named(tallies, turn):
        used = int((tallies > 0).sum())
        fixed = max(1, used // 4)
        moved = fixed + (places - fixed + turn * (used - fixed)) % max(1, amount - fixed)
        return jnp.zeros((amount,), jnp.int32).at[sequence[jnp.where(places < fixed, places, moved)]].set(jnp.asarray(tallies, jnp.int32))

    tallies = jnp.where(number % 4 == 0, named(crowded, number // 4), named(common, number - number // 4 - 1))
    mixed = jax.random.permutation(jax.random.fold_in(own, 3), amount)
    donor, taker = mixed[0:amount // 2 * 2:2], mixed[1:amount // 2 * 2:2]
    margin = jnp.minimum(tallies[donor] - 1, reach - tallies[taker]) // 2
    margin = jnp.where((donor == sequence[0]) | (taker == sequence[0]) | (tallies[taker] == 0), 0, jnp.maximum(margin, 0))
    moved = jax.random.randint(jax.random.fold_in(own, 4), (amount // 2,), 0, 1 << 20) % (margin + 1)
    tallies = tallies.at[donor].add(-moved).at[taker].add(moved)
    members = jnp.searchsorted(jnp.cumsum(tallies), jnp.arange(rows * top), side="right").astype(jnp.int32)
    table = members.reshape(top, rows).T
    table = table[jax.random.permutation(jax.random.fold_in(own, 1), rows)]
    turn = jax.random.randint(jax.random.fold_in(own, 2), (rows, 1), 0, top)
    return jnp.take_along_axis(table, (jnp.arange(top)[None, :] + turn) % top, axis=1)


def load_shares(number_of, total, limit, lean, full):
    loads = [(1 << 20) // math.isqrt(grade ** lean) + 1 for grade in range(1, number_of + 1)]
    largest = limit if full else min(limit, max(-(-total // number_of), total * loads[0] // sum(loads)))
    least = 1 if total - largest >= number_of - 1 else 0
    holding, rest = [largest] + [least] * (number_of - 1), total - largest - least * (number_of - 1)
    while rest > 0:
        free = [i for i in range(1, number_of) if holding[i] < largest] or [i for i in range(1, number_of) if holding[i] < limit]
        pool, remaining = sum([loads[i] for i in free]), rest
        for i in free:
            addition = min(limit - holding[i], max(1, remaining * loads[i] // pool), rest)
            holding[i] = holding[i] + addition
            rest = rest - addition
    return np.array(holding)


def centred(own_key, dims, deviation, bound, pieces=(), held_as=jnp.bfloat16):
    entries = jax.random.normal(own_key, dims, jnp.float32) * deviation
    if len(pieces) > 0:
        entries = block_scale(own_key, dims, pieces, -0.22, 0.18) * entries
    return jnp.clip(entries, min=-bound, max=bound).astype(held_as)


def setup_inputs(seed: int = 0) -> dict:
    seeds = jax.random.split(jax.random.key(seed), 7)
    output_grad = centred(seeds[0], (TOKENS, D), 1.0, 6.0, ((0, 16), (1, 64)))
    routing_keys = jax.random.split(jax.random.fold_in(seeds[1], 1), TOKENS // TOK_DEV)
    routing_turns = jax.random.permutation(jax.random.fold_in(seeds[1], 3), TOKENS // TOK_DEV)
    routing = jax.vmap(lambda own, number: shared_out(jax.random.fold_in(seeds[1], 2), own, number, TOK_DEV, EXPERTS, TOPK, CAP, 2))(routing_keys, routing_turns).reshape((TOKENS, TOPK))
    gates = jnp.clip(jnp.exp(math.log(1.0) - 2.3025851 * jax.random.uniform(seeds[2], (TOKENS, TOPK), jnp.float32) ** block_scale(seeds[2], (TOKENS, TOPK), ((0, 16),), -0.2, 0.2)), 0.1, 1.0)
    saved_inputs = centred(seeds[3], (EXPERTS, SLOTS, D), 1.0, 6.0, ((0, 16), (2, 64)))
    gate_up = centred(seeds[4], (EXPERTS, D, 2 * F), D ** -0.5, 0.0625, ((0, 16), (1, 64)))
    down_weight = centred(seeds[5], (EXPERTS, F, D), D ** -0.5, 0.0625, ((0, 16), (2, 64)))
    return {"output_grad": output_grad, "routing": routing, "gates": gates, "saved_inputs": saved_inputs, "gate_up": gate_up, "down_weight": down_weight}


def slot_table(route_ids):
    flat_ids = route_ids.reshape(-1)
    expert_ids = jnp.arange(EXPERTS, dtype=jnp.int32)
    onehot = (flat_ids[:, None] == expert_ids[None, :]).astype(jnp.int32)
    earlier = jnp.cumsum(onehot, axis=0) - onehot
    rank_in = jnp.sum(earlier * onehot, axis=1)
    slot_id = flat_ids * CAP + rank_in
    slot_ids = jnp.arange(EXPERTS * CAP, dtype=jnp.int32)
    return (slot_id[:, None] == slot_ids[None, :]).astype(jnp.float32)


def one_expert(operands):
    inputs_here, received_here, weights_up, weights_down = operands
    inputs_here = inputs_here.astype(jnp.float32)
    weights_up = weights_up.astype(jnp.float32)
    projected = jnp.dot(inputs_here, weights_up, precision=lax.Precision.HIGHEST)
    gate_pre = projected[:, :F]
    up_pre = projected[:, F:]
    hidden_grad = jnp.dot(received_here.astype(jnp.float32), weights_down.astype(jnp.float32).T, precision=lax.Precision.HIGHEST)
    sigmoid_gate = jax.nn.sigmoid(gate_pre)
    slope = sigmoid_gate * (1.0 + gate_pre * (1.0 - sigmoid_gate))
    pre_grad = jnp.concatenate([hidden_grad * up_pre * slope, hidden_grad * gate_pre * sigmoid_gate], axis=-1).astype(jnp.bfloat16)
    pre_float = pre_grad.astype(jnp.float32)
    weight_grad = jnp.dot(inputs_here.T, pre_float, precision=lax.Precision.HIGHEST).astype(jnp.bfloat16)
    slot_grad = jnp.dot(pre_float, weights_up.T, precision=lax.Precision.HIGHEST).astype(jnp.bfloat16)
    return weight_grad, slot_grad


def reference(output_grad, routing, gates, saved_inputs, gate_up, down_weight):
    grads_all = output_grad.reshape(N_EXPERT, TOK_DEV, D).astype(jnp.float32)
    gates_all = gates.reshape(N_EXPERT, TOK_DEV, TOPK)
    routed = (gates_all[..., None] * grads_all[:, :, None, :]).astype(jnp.bfloat16)
    routed = routed.reshape(N_EXPERT, TOK_DEV * TOPK, D)
    tables = jax.vmap(slot_table)(routing.reshape(N_EXPERT, TOK_DEV * TOPK))
    sent = jnp.einsum('srk,srd->skd', tables, routed.astype(jnp.float32)).astype(jnp.bfloat16)
    received = sent.reshape(N_EXPERT, EXPERTS, CAP, D).transpose(1, 0, 2, 3).reshape(EXPERTS, SLOTS, D)
    gate_up_grad, slot_grad = lax.map(one_expert, (saved_inputs, received, gate_up, down_weight))
    returned_rows = slot_grad.reshape(EXPERTS, N_EXPERT, CAP, D).transpose(1, 0, 2, 3).reshape(N_EXPERT, EXPERTS * CAP, D)
    token_grads = jnp.einsum('srk,skd->srd', tables, returned_rows.astype(jnp.float32))
    input_grad = token_grads.reshape(N_EXPERT, TOK_DEV, TOPK, D).sum(axis=2).astype(jnp.bfloat16).reshape(TOKENS, D)
    return input_grad, gate_up_grad
```

```python
import jax
import jax.numpy as jnp
from jax import lax
from jax.experimental import pallas as pl
from jax.experimental.pallas import tpu as pltpu
from jax.sharding import PartitionSpec as P

BF16 = jnp.bfloat16
F32 = jnp.float32
SIDE = 8
PEERS = 16
MINE = 3
SLOTS = 64
TILE = 256


def kernel(
    og_ref, rt_ref, gt_ref, x_ref, w_ref, d_ref,
    ig_ref, wg_ref,
    og_pad, rt_pad, gt_pad, table,
    e1_send, e1_recv, got, gu_send, gu_recv, h_send, h_recv, s2_send, s2_recv,
    gath, pre, slot_rows, e2_send, e2_recv,
    e_sems, r_sems, s_sems,
):
    ex = lax.axis_index("expert")
    dp = lax.axis_index("dp")
    z = dp // SIDE
    x = dp % SIDE
    even = ex % 2 == 0
    first = jnp.where(even, x, z)
    second = jnp.where(even, z, x)
    first_step = jnp.where(even, 1, SIDE)
    second_step = jnp.where(even, SIDE, 1)

    def along_first(k):
        to = (first + k) % SIDE
        return (ex, dp + (to - first) * first_step), to

    def along_second(k):
        to = (second + k) % SIDE
        return (ex, dp + (to - second) * second_step), to

    def along_expert(k):
        to = (ex + k) % PEERS
        return (to, dp), to

    barrier = pltpu.get_barrier_semaphore()

    def greet(who, count):
        @pl.loop(1, count)
        def _(k):
            pl.semaphore_signal(
                barrier, inc=1, device_id=who(k)[0], device_id_type=pl.DeviceIdType.MESH
            )

    greet(along_first, SIDE)
    greet(along_second, SIDE)
    greet(along_expert, PEERS)

    def send(src, dst, send_sem, recv_sem, device):
        pltpu.make_async_remote_copy(
            src_ref=src, dst_ref=dst, send_sem=send_sem, recv_sem=recv_sem,
            device_id=device, device_id_type=pl.DeviceIdType.MESH,
        ).start()

    def wait(ref, sem):
        pltpu.make_async_copy(ref, ref, sem).wait()

    og_pad[...] = jnp.zeros_like(og_pad)
    og_pad[0:12, 0:112] = og_ref[...]
    rt_pad[...] = jnp.full_like(rt_pad, -2)
    rt_pad[:, 0:12] = rt_ref[...]
    gt_pad[...] = jnp.zeros_like(gt_pad)
    gt_pad[:, 0:12] = gt_ref[...]
    shape = (PEERS * 16, 128)
    row = lax.broadcasted_iota(jnp.int32, shape, 0)
    which = (row >> 2) & 3
    expert_id = jnp.where(which < MINE, (row >> 4) * MINE + which, -1)
    names = jnp.zeros(shape, F32)
    gate = jnp.zeros(shape, F32)
    for k in range(8):
        hit = rt_pad[k : k + 1, :] == expert_id
        names = names + jnp.where(hit, 1.0, 0.0)
        gate = gate + jnp.where(hit, gt_pad[k : k + 1, :], 0.0)
    before = lax.broadcasted_iota(jnp.int32, (128, 128), 0) < lax.broadcasted_iota(
        jnp.int32, (128, 128), 1
    )
    rank = jnp.dot(
        names.astype(BF16), jnp.where(before, 1.0, 0.0).astype(BF16), preferred_element_type=F32
    )
    fills = jnp.where(rank == (row & 3).astype(F32), names, 0.0)
    gate_of = jnp.sum(fills * gate, axis=1, keepdims=True)
    table[...] = fills.astype(BF16)
    rows_out = jnp.dot(table[...], og_pad[...], preferred_element_type=F32) * gate_of
    e1_send[...] = rows_out.astype(BF16).reshape(PEERS, 16, 128)

    for e in range(MINE):
        for n in range(2048 // TILE):
            part = jnp.dot(
                x_ref[e], w_ref[e, :, n * TILE : (n + 1) * TILE], preferred_element_type=F32
            ).astype(BF16)
            kind, at = divmod(n * TILE, 1024)
            for i in range(TILE // 128):
                gu_send[at // 128 + i, e, kind * SLOTS : (kind + 1) * SLOTS, :] = part[
                    :, i * 128 : (i + 1) * 128
                ]

    pl.semaphore_wait(barrier, 2 * (SIDE - 1) + PEERS - 1)

    @pl.loop(1, PEERS)
    def _(k):
        device, to = along_expert(k)
        send(e1_send.at[to], e1_recv.at[ex], e_sems.at[0], e_sems.at[1], device)

    e1_recv[ex] = e1_send[ex]

    for e in range(MINE):

        @pl.loop(1, SIDE)
        def _(k):
            device, to = along_first(k)
            send(gu_send.at[to, e], gu_recv.at[e, k - 1], s_sems.at[0, e], r_sems.at[0, e], device)

    wait(e1_recv.at[0 : PEERS - 1], e_sems.at[1])
    take = lax.broadcasted_iota(jnp.int32, (MINE * SLOTS, 256), 0)
    lane = lax.broadcasted_iota(jnp.int32, (MINE * SLOTS, 256), 1)
    source = ((take >> 2) & 15) * 16 + (take >> 6) * 4 + (take & 3)
    pick = jnp.where(lane == source, 1.0, 0.0).astype(BF16)
    got[...] = jnp.dot(
        pick, e1_recv[...].reshape(PEERS * 16, 128), preferred_element_type=F32
    ).astype(BF16)
    for e in range(MINE):
        for n in range(1024 // TILE):
            part = jnp.dot(
                got[e * SLOTS : (e + 1) * SLOTS, 0:112],
                d_ref[e, :, n * TILE : (n + 1) * TILE],
                preferred_element_type=F32,
            ).astype(BF16)
            for i in range(TILE // 128):
                h_send[n * TILE // 128 + i, e] = part[:, i * 128 : (i + 1) * 128]

        @pl.loop(1, SIDE)
        def _(k):
            device, to = along_first(k)
            send(h_send.at[to, e], h_recv.at[e, k - 1], s_sems.at[1, e], r_sems.at[1, e], device)

    for e in range(MINE):
        wait(gu_recv.at[e], r_sems.at[0, e])
        total = gu_send[first, e].astype(F32)
        for k in range(SIDE - 1):
            total = total + gu_recv[e, k].astype(F32)
        s2_send[:, e, 0:8, :] = total[0:SLOTS].reshape(SIDE, 8, 128)
        s2_send[:, e, 8:16, :] = total[SLOTS:].reshape(SIDE, 8, 128)
        wait(h_recv.at[e], r_sems.at[1, e])
        total = h_send[first, e].astype(F32)
        for k in range(SIDE - 1):
            total = total + h_recv[e, k].astype(F32)
        s2_send[:, e, 16:24, :] = total.reshape(SIDE, 8, 128)

        @pl.loop(1, SIDE)
        def _(k):
            device, to = along_second(k)
            send(s2_send.at[to, e], s2_recv.at[e, k - 1], s_sems.at[2, e], r_sems.at[2, e], device)

    for e in range(MINE):
        wait(s2_recv.at[e], r_sems.at[2, e])
        total = s2_send[second, e]
        for k in range(SIDE - 1):
            total = total + s2_recv[e, k]
        gate_pre, up_pre, hidden = total[0:8], total[8:16], total[16:24]
        sg = 1.0 / (1.0 + jnp.exp(-gate_pre))
        slope = sg * (1.0 + gate_pre * (1.0 - sg))
        both = jnp.concatenate([hidden * up_pre * slope, hidden * gate_pre * sg], axis=0)
        gath[e, first, second] = both.astype(BF16)

        @pl.loop(1, SIDE)
        def _(k):
            device, _to = along_second(k)
            here = gath.at[e, first, second]
            send(here, here, s_sems.at[3, e], r_sems.at[3, e], device)

    for e in range(MINE):
        wait(gath.at[e, 0, 0 : SIDE - 1], r_sems.at[3, e])

        @pl.loop(1, SIDE)
        def _(k):
            device, _to = along_first(k)
            here = gath.at[e, first]
            send(here, here, s_sems.at[4, e], r_sems.at[4, e], device)

    slot_rows[...] = jnp.zeros_like(slot_rows)
    for e in range(MINE):
        wait(gath.at[e, 0 : SIDE - 1], r_sems.at[4, e])
        for j in range(SIDE):
            block = gath[e, j].astype(F32)
            pre[e, :, j * 128 : (j + 1) * 128] = block[:, 0:8].reshape(SLOTS, 128).astype(BF16)
            pre[e, :, 1024 + j * 128 : 1024 + (j + 1) * 128] = (
                block[:, 8:16].reshape(SLOTS, 128).astype(BF16)
            )
        slot_rows[e * SLOTS : (e + 1) * SLOTS, 0:112] = lax.dot_general(
            pre[e], w_ref[e], (((1,), (1,)), ((), ())), preferred_element_type=F32
        ).astype(BF16)
    back = lax.broadcasted_iota(jnp.int32, (256, 256), 0)
    lane = lax.broadcasted_iota(jnp.int32, (256, 256), 1)
    source = jnp.where(
        ((back >> 2) & 3) < MINE, ((back >> 2) & 3) * SLOTS + (back >> 4) * 4 + (back & 3), -1
    )
    e2_send[...] = (
        jnp.dot(
            jnp.where(lane == source, 1.0, 0.0).astype(BF16),
            slot_rows[...],
            preferred_element_type=F32,
        )
        .astype(BF16)
        .reshape(PEERS, 16, 128)
    )

    @pl.loop(1, PEERS)
    def _(k):
        device, to = along_expert(k)
        send(e2_send.at[to], e2_recv.at[ex], e_sems.at[2], e_sems.at[3], device)

    e2_recv[ex] = e2_send[ex]

    for e in range(MINE):
        for n in range(2048 // TILE):
            cols = slice(n * TILE, (n + 1) * TILE)
            wg_ref[e, :, cols] = lax.dot_general(
                x_ref[e], pre[e, :, cols], (((0,), (0,)), ((), ())), preferred_element_type=F32
            ).astype(BF16)

    wait(e2_recv.at[0 : PEERS - 1], e_sems.at[3])
    token = lax.dot_general(
        table[...],
        e2_recv[...].reshape(PEERS * 16, 128),
        (((0,), (0,)), ((), ())),
        preferred_element_type=F32,
    )
    ig_ref[...] = token[0:12, 0:112].astype(BF16)

    wait(e1_send.at[0 : PEERS - 1], e_sems.at[0])
    wait(e2_send.at[0 : PEERS - 1], e_sems.at[2])
    for e in range(MINE):
        wait(gu_recv.at[e], s_sems.at[0, e])
        wait(h_recv.at[e], s_sems.at[1, e])
        wait(s2_recv.at[e], s_sems.at[2, e])
        wait(gath.at[e, 0, 0 : SIDE - 1], s_sems.at[3, e])
        wait(gath.at[e, 0 : SIDE - 1], s_sems.at[4, e])


def body(output_grad, routing, gates, saved_inputs, gate_up, down_weight):
    vmem = pl.BlockSpec(memory_space=pltpu.VMEM)
    dma = pltpu.SemaphoreType.DMA
    return pl.pallas_call(
        kernel,
        out_shape=(
            jax.ShapeDtypeStruct(output_grad.shape, BF16),
            jax.ShapeDtypeStruct(gate_up.shape, BF16),
        ),
        in_specs=[vmem] * 6,
        out_specs=(vmem, vmem),
        scratch_shapes=[
            pltpu.VMEM((128, 128), BF16),
            pltpu.VMEM((8, 128), jnp.int32),
            pltpu.VMEM((8, 128), F32),
            pltpu.VMEM((256, 128), BF16),
            pltpu.VMEM((PEERS, 16, 128), BF16),
            pltpu.VMEM((PEERS, 16, 128), BF16),
            pltpu.VMEM((MINE * SLOTS, 128), BF16),
            pltpu.VMEM((SIDE, MINE, 2 * SLOTS, 128), BF16),
            pltpu.VMEM((MINE, SIDE - 1, 2 * SLOTS, 128), BF16),
            pltpu.VMEM((SIDE, MINE, SLOTS, 128), BF16),
            pltpu.VMEM((MINE, SIDE - 1, SLOTS, 128), BF16),
            pltpu.VMEM((SIDE, MINE, 24, 128), F32),
            pltpu.VMEM((MINE, SIDE - 1, 24, 128), F32),
            pltpu.VMEM((MINE, SIDE, SIDE, 16, 128), BF16),
            pltpu.VMEM((MINE, SLOTS, 2048), BF16),
            pltpu.VMEM((256, 128), BF16),
            pltpu.VMEM((PEERS, 16, 128), BF16),
            pltpu.VMEM((PEERS, 16, 128), BF16),
            dma((4,)),
            dma((5, MINE)),
            dma((5, MINE)),
        ],
        compiler_params=pltpu.CompilerParams(
            collective_id=1, has_side_effects=True, vmem_limit_bytes=48 << 20
        ),
    )(
        output_grad,
        routing.T,
        gates.T,
        saved_inputs,
        gate_up,
        jnp.swapaxes(down_weight, 1, 2),
    )


def solution(mesh):
    placed = (
        P("expert", "dp"),
        P("expert", None),
        P("expert", None),
        P("expert", None, "dp"),
        P("expert", "dp", None),
        P("expert", None, "dp"),
    )
    return jax.shard_map(
        body,
        mesh=mesh,
        in_specs=placed,
        out_specs=(P("expert", "dp"), P("expert", "dp", None)),
        check_vma=False,
    )
```

```python
import jax
import jax.numpy as jnp
from jax import lax
from jax.experimental import pallas as pl
from jax.experimental.pallas import tpu as pltpu
from jax.sharding import PartitionSpec as P

BF16 = jnp.bfloat16
F32 = jnp.float32
SIDE = 8
PEERS = 16
MINE = 3
SLOTS = 64
TILE = 256


def kernel(
    og_hbm, rt_hbm, gt_hbm, x_hbm, w_hbm, d_hbm,
    ig_hbm, wg_hbm,
    ig_ref, wg_ref, out_sems,
    og_ref, rt_ref, gt_ref, x_ref, w_ref, d_ref, in_sems,
    og_pad, rt_pad, gt_pad, table,
    e1_send, e1_recv, got, gu_send, gu_recv, far3, far4, passed, h_send, h_recv, s2_send, s2_recv,
    gath, pre, slot_rows, e2_send, e2_recv,
    e_sems, r_sems, s_sems, ready,
):
    ex = lax.axis_index("expert")
    dp = lax.axis_index("dp")
    z = dp // SIDE
    x = dp % SIDE
    even = ex % 2 == 0
    first = jnp.where(even, x, z)
    second = jnp.where(even, z, x)
    first_step = jnp.where(even, 1, SIDE)
    second_step = jnp.where(even, SIDE, 1)

    def along_first(k):
        to = (first + k) % SIDE
        return (ex, dp + (to - first) * first_step), to

    def along_second(k):
        to = (second + k) % SIDE
        return (ex, dp + (to - second) * second_step), to

    def along_expert(k):
        to = (ex + k) % PEERS
        return (to, dp), to

    barrier = pltpu.get_barrier_semaphore()

    def greet(who, count):
        @pl.loop(1, count)
        def _(k):
            pl.semaphore_signal(
                barrier, inc=1, device_id=who(k)[0], device_id_type=pl.DeviceIdType.MESH
            )

    loads = {
        "x": (x_hbm, x_ref), "w0": (w_hbm.at[0], w_ref.at[0]), "w1": (w_hbm.at[1], w_ref.at[1]),
        "w2": (w_hbm.at[2], w_ref.at[2]), "og": (og_hbm, og_ref), "rt": (rt_hbm, rt_ref),
        "gt": (gt_hbm, gt_ref), "d": (d_hbm, d_ref),
    }
    loads = {
        name: pltpu.make_async_copy(src, dst, in_sems.at[i])
        for i, (name, (src, dst)) in enumerate(loads.items())
    }
    for load in loads.values():
        load.start()
    def along_x(k):
        to = (x + k) % SIDE
        return (ex, z * SIDE + to), to

    def at_z(to):
        return (ex, to * SIDE + x)

    greet(along_expert, PEERS)
    greet(along_x, SIDE)

    @pl.loop(z + 1, SIDE)
    def _(to):
        pl.semaphore_signal(
            barrier, inc=1, device_id=at_z(to), device_id_type=pl.DeviceIdType.MESH
        )

    def await_ready(k, turn):
        to = (z + k) % SIDE

        @pl.when(jnp.logical_and(turn, to > z))
        def _():
            pl.semaphore_wait(ready.at[to], 1)

    def send(src, dst, send_sem, recv_sem, device):
        pltpu.make_async_remote_copy(
            src_ref=src, dst_ref=dst, send_sem=send_sem, recv_sem=recv_sem,
            device_id=device, device_id_type=pl.DeviceIdType.MESH,
        ).start()

    def wait(ref, sem):
        pltpu.make_async_copy(ref, ref, sem).wait()

    loads["x"].wait()
    for e in range(MINE):
        loads[f"w{e}"].wait()
        for n in range(2048 // TILE):
            part = jnp.dot(
                x_ref[e], w_ref[e, :, n * TILE : (n + 1) * TILE], preferred_element_type=F32
            ).astype(BF16)
            kind, at = divmod(n * TILE, 1024)
            for i in range(TILE // 128):
                gu_send[at // 128 + i, e, kind * SLOTS : (kind + 1) * SLOTS, :] = part[
                    :, i * 128 : (i + 1) * 128
                ]

    for name in ("og", "rt", "gt"):
        loads[name].wait()
    og_pad[...] = jnp.zeros_like(og_pad)
    og_pad[0:12, 0:112] = og_ref[...]
    rt_pad[...] = jnp.full_like(rt_pad, -2)
    rt_pad[:, 0:12] = rt_ref[...]
    gt_pad[...] = jnp.zeros_like(gt_pad)
    gt_pad[:, 0:12] = gt_ref[...]
    shape = (PEERS * 16, 128)
    row = lax.broadcasted_iota(jnp.int32, shape, 0)
    which = (row >> 2) & 3
    expert_id = jnp.where(which < MINE, (row >> 4) * MINE + which, -1)
    names = jnp.zeros(shape, F32)
    gate = jnp.zeros(shape, F32)
    for k in range(8):
        hit = rt_pad[k : k + 1, :] == expert_id
        names = names + jnp.where(hit, 1.0, 0.0)
        gate = gate + jnp.where(hit, gt_pad[k : k + 1, :], 0.0)
    before = lax.broadcasted_iota(jnp.int32, (128, 128), 0) < lax.broadcasted_iota(
        jnp.int32, (128, 128), 1
    )
    rank = jnp.dot(
        names.astype(BF16), jnp.where(before, 1.0, 0.0).astype(BF16), preferred_element_type=F32
    )
    fills = jnp.where(rank == (row & 3).astype(F32), names, 0.0)
    gate_of = jnp.sum(fills * gate, axis=1, keepdims=True)
    table[...] = fills.astype(BF16)
    rows_out = jnp.dot(table[...], og_pad[...], preferred_element_type=F32) * gate_of
    e1_send[...] = rows_out.astype(BF16).reshape(PEERS, 16, 128)

    pl.semaphore_wait(barrier, SIDE - 1 + PEERS - 1 + z)

    @pl.loop(0, z)
    def _(to):
        pl.semaphore_signal(
            ready.at[z], inc=1, device_id=at_z(to), device_id_type=pl.DeviceIdType.MESH
        )

    @pl.loop(1, PEERS)
    def _(k):
        device, to = along_expert(k)
        send(e1_send.at[to], e1_recv.at[ex], e_sems.at[0], e_sems.at[1], device)

    e1_recv[ex] = e1_send[ex]

    odd = jnp.logical_not(even)
    for side, way in ((1, 1), (0, -1)):
        one, next_one = along_first(way)
        two, _ = along_first(2 * way)
        _, third = along_first(3 * way)
        _, fourth = along_first(4)
        half = pl.ds(side * SLOTS, SLOTS)
        await_ready(way, odd)
        for e in range(MINE):
            send(gu_send.at[third, e], far3.at[e, side], s_sems.at[5, e], r_sems.at[5, e], one)
        await_ready(2 * way, odd)
        for e in range(MINE):
            send(
                gu_send.at[fourth, e, half], far4.at[e, side],
                s_sems.at[6, e], r_sems.at[6, e], two,
            )
        for e in range(MINE):
            send(gu_send.at[next_one, e], gu_recv.at[e, side], s_sems.at[0, e], r_sems.at[0, e], one)
    for e in range(MINE):
        wait(far3.at[e], r_sems.at[5, e])
        wait(far4.at[e], r_sems.at[6, e])
        for side, way in enumerate((-1, 1)):
            two, second_one = along_first(2 * way)
            total = gu_send[second_one, e].astype(F32) + far3[e, side].astype(F32)
            extra = far4[e, side].astype(F32)
            parts = [total[0:SLOTS], total[SLOTS:]]
            parts[side] = parts[side] + extra
            passed[e, side, 0:SLOTS] = parts[0].astype(BF16)
            passed[e, side, SLOTS:] = parts[1].astype(BF16)
            send(passed.at[e, side], gu_recv.at[e, 2 + side], s_sems.at[0, e], r_sems.at[0, e], two)

    loads["d"].wait()
    wait(e1_recv.at[0 : PEERS - 1], e_sems.at[1])
    take = lax.broadcasted_iota(jnp.int32, (MINE * SLOTS, 256), 0)
    lane = lax.broadcasted_iota(jnp.int32, (MINE * SLOTS, 256), 1)
    source = ((take >> 2) & 15) * 16 + (take >> 6) * 4 + (take & 3)
    pick = jnp.where(lane == source, 1.0, 0.0).astype(BF16)
    got[...] = jnp.dot(
        pick, e1_recv[...].reshape(PEERS * 16, 128), preferred_element_type=F32
    ).astype(BF16)
    for k in (3, 4, 5):
        await_ready(k, odd)
    for e in range(MINE):
        for n in range(1024 // TILE):
            part = jnp.dot(
                got[e * SLOTS : (e + 1) * SLOTS, 0:112],
                d_ref[e, :, n * TILE : (n + 1) * TILE],
                preferred_element_type=F32,
            ).astype(BF16)
            for i in range(TILE // 128):
                h_send[n * TILE // 128 + i, e] = part[:, i * 128 : (i + 1) * 128]

        @pl.loop(1, SIDE)
        def _(k):
            device, to = along_first(k)
            send(h_send.at[to, e], h_recv.at[e, k - 1], s_sems.at[1, e], r_sems.at[1, e], device)

    for k in range(1, SIDE):
        await_ready(k, even)
    for e in range(MINE):
        wait(gu_recv.at[e], r_sems.at[0, e])
        total = gu_send[first, e].astype(F32)
        for k in range(4):
            total = total + gu_recv[e, k].astype(F32)
        s2_send[:, e, 0:8, :] = total[0:SLOTS].reshape(SIDE, 8, 128)
        s2_send[:, e, 8:16, :] = total[SLOTS:].reshape(SIDE, 8, 128)
        wait(h_recv.at[e], r_sems.at[1, e])
        total = h_send[first, e].astype(F32)
        for k in range(SIDE - 1):
            total = total + h_recv[e, k].astype(F32)
        s2_send[:, e, 16:24, :] = total.reshape(SIDE, 8, 128)

        @pl.loop(1, SIDE)
        def _(k):
            device, to = along_second(k)
            send(s2_send.at[to, e], s2_recv.at[e, k - 1], s_sems.at[2, e], r_sems.at[2, e], device)

    for e in range(MINE):
        wait(s2_recv.at[e], r_sems.at[2, e])
        total = s2_send[second, e]
        for k in range(SIDE - 1):
            total = total + s2_recv[e, k]
        gate_pre, up_pre, hidden = total[0:8], total[8:16], total[16:24]
        sg = 1.0 / (1.0 + jnp.exp(-gate_pre))
        slope = sg * (1.0 + gate_pre * (1.0 - sg))
        both = jnp.concatenate([hidden * up_pre * slope, hidden * gate_pre * sg], axis=0)
        gath[e, first, second] = both.astype(BF16)

        @pl.loop(1, SIDE)
        def _(k):
            device, _to = along_second(k)
            here = gath.at[e, first, second]
            send(here, here, s_sems.at[3, e], r_sems.at[3, e], device)

    for e in range(MINE):
        wait(gath.at[e, 0, 0 : SIDE - 1], r_sems.at[3, e])

        @pl.loop(1, SIDE)
        def _(k):
            device, _to = along_first(k)
            here = gath.at[e, first]
            send(here, here, s_sems.at[4, e], r_sems.at[4, e], device)

    slot_rows[...] = jnp.zeros_like(slot_rows)
    for e in range(MINE):
        wait(gath.at[e, 0 : SIDE - 1], r_sems.at[4, e])
        for j in range(SIDE):
            block = gath[e, j].astype(F32)
            pre[e, :, j * 128 : (j + 1) * 128] = block[:, 0:8].reshape(SLOTS, 128).astype(BF16)
            pre[e, :, 1024 + j * 128 : 1024 + (j + 1) * 128] = (
                block[:, 8:16].reshape(SLOTS, 128).astype(BF16)
            )
        slot_rows[e * SLOTS : (e + 1) * SLOTS, 0:112] = lax.dot_general(
            pre[e], w_ref[e], (((1,), (1,)), ((), ())), preferred_element_type=F32
        ).astype(BF16)
    back = lax.broadcasted_iota(jnp.int32, (256, 256), 0)
    lane = lax.broadcasted_iota(jnp.int32, (256, 256), 1)
    source = jnp.where(
        ((back >> 2) & 3) < MINE, ((back >> 2) & 3) * SLOTS + (back >> 4) * 4 + (back & 3), -1
    )
    e2_send[...] = (
        jnp.dot(
            jnp.where(lane == source, 1.0, 0.0).astype(BF16),
            slot_rows[...],
            preferred_element_type=F32,
        )
        .astype(BF16)
        .reshape(PEERS, 16, 128)
    )

    @pl.loop(1, PEERS)
    def _(k):
        device, to = along_expert(k)
        send(e2_send.at[to], e2_recv.at[ex], e_sems.at[2], e_sems.at[3], device)

    e2_recv[ex] = e2_send[ex]

    for e in range(MINE):
        for n in range(2048 // TILE):
            cols = slice(n * TILE, (n + 1) * TILE)
            wg_ref[e, :, cols] = lax.dot_general(
                x_ref[e], pre[e, :, cols], (((0,), (0,)), ((), ())), preferred_element_type=F32
            ).astype(BF16)
        pltpu.make_async_copy(wg_ref.at[e], wg_hbm.at[e], out_sems.at[e]).start()

    wait(e2_recv.at[0 : PEERS - 1], e_sems.at[3])
    token = lax.dot_general(
        table[...],
        e2_recv[...].reshape(PEERS * 16, 128),
        (((0,), (0,)), ((), ())),
        preferred_element_type=F32,
    )
    ig_ref[...] = token[0:12, 0:112].astype(BF16)
    last = pltpu.make_async_copy(ig_ref, ig_hbm, out_sems.at[MINE])
    last.start()

    for e in range(MINE):
        pltpu.make_async_copy(wg_ref.at[e], wg_hbm.at[e], out_sems.at[e]).wait()
    last.wait()
    wait(e1_send.at[0 : PEERS - 1], e_sems.at[0])
    wait(e2_send.at[0 : PEERS - 1], e_sems.at[2])
    for e in range(MINE):
        wait(gu_recv.at[e], s_sems.at[0, e])
        wait(far3.at[e], s_sems.at[5, e])
        wait(far4.at[e], s_sems.at[6, e])
        wait(h_recv.at[e], s_sems.at[1, e])
        wait(s2_recv.at[e], s_sems.at[2, e])
        wait(gath.at[e, 0, 0 : SIDE - 1], s_sems.at[3, e])
        wait(gath.at[e, 0 : SIDE - 1], s_sems.at[4, e])


def body(output_grad, routing, gates, saved_inputs, gate_up, down_weight):
    dma = pltpu.SemaphoreType.DMA
    return pl.pallas_call(
        kernel,
        out_shape=(
            jax.ShapeDtypeStruct(output_grad.shape, BF16),
            jax.ShapeDtypeStruct(gate_up.shape, BF16),
        ),
        in_specs=[pl.BlockSpec(memory_space=pl.ANY)] * 6,
        out_specs=(pl.BlockSpec(memory_space=pl.ANY),) * 2,
        scratch_shapes=[
            pltpu.VMEM((12, 112), BF16),
            pltpu.VMEM((MINE, 112, 2048), BF16),
            dma((MINE + 1,)),
            pltpu.VMEM((12, 112), BF16),
            pltpu.VMEM((8, 12), jnp.int32),
            pltpu.VMEM((8, 12), F32),
            pltpu.VMEM((MINE, SLOTS, 112), BF16),
            pltpu.VMEM((MINE, 112, 2048), BF16),
            pltpu.VMEM((MINE, 112, 1024), BF16),
            dma((8,)),
            pltpu.VMEM((128, 128), BF16),
            pltpu.VMEM((8, 128), jnp.int32),
            pltpu.VMEM((8, 128), F32),
            pltpu.VMEM((256, 128), BF16),
            pltpu.VMEM((PEERS, 16, 128), BF16),
            pltpu.VMEM((PEERS, 16, 128), BF16),
            pltpu.VMEM((MINE * SLOTS, 128), BF16),
            pltpu.VMEM((SIDE, MINE, 2 * SLOTS, 128), BF16),
            pltpu.VMEM((MINE, 4, 2 * SLOTS, 128), BF16),
            pltpu.VMEM((MINE, 2, 2 * SLOTS, 128), BF16),
            pltpu.VMEM((MINE, 2, SLOTS, 128), BF16),
            pltpu.VMEM((MINE, 2, 2 * SLOTS, 128), BF16),
            pltpu.VMEM((SIDE, MINE, SLOTS, 128), BF16),
            pltpu.VMEM((MINE, SIDE - 1, SLOTS, 128), BF16),
            pltpu.VMEM((SIDE, MINE, 24, 128), F32),
            pltpu.VMEM((MINE, SIDE - 1, 24, 128), F32),
            pltpu.VMEM((MINE, SIDE, SIDE, 16, 128), BF16),
            pltpu.VMEM((MINE, SLOTS, 2048), BF16),
            pltpu.VMEM((256, 128), BF16),
            pltpu.VMEM((PEERS, 16, 128), BF16),
            pltpu.VMEM((PEERS, 16, 128), BF16),
            dma((4,)),
            dma((7, MINE)),
            dma((7, MINE)),
            pltpu.SemaphoreType.REGULAR((SIDE,)),
        ],
        compiler_params=pltpu.CompilerParams(
            collective_id=1, has_side_effects=True, vmem_limit_bytes=60 << 20
        ),
    )(
        output_grad,
        routing.T,
        gates.T,
        saved_inputs,
        gate_up,
        jnp.swapaxes(down_weight, 1, 2),
    )


def solution(mesh):
    placed = (
        P("expert", "dp"),
        P("expert", None),
        P("expert", None),
        P("expert", None, "dp"),
        P("expert", "dp", None),
        P("expert", None, "dp"),
    )
    return jax.shard_map(
        body,
        mesh=mesh,
        in_specs=placed,
        out_specs=(P("expert", "dp"), P("expert", "dp", None)),
        check_vma=False,
    )
```

```python
import jax
import jax.numpy as jnp
from jax import lax
from jax.experimental import pallas as pl
from jax.experimental.pallas import tpu as pltpu
from jax.sharding import PartitionSpec as P

BF16 = jnp.bfloat16
F32 = jnp.float32
SIDE = 8
PEERS = 16
MINE = 3
SLOTS = 64
TILE = 256


def kernel(
    og_hbm, rt_hbm, gt_hbm, x_hbm, w_hbm, d_hbm,
    ig_ref, wg_ref,
    og_ref, rt_ref, gt_ref, x_ref, w_ref, d_ref, in_sems,
    og_pad, rt_pad, gt_pad, table,
    e1_send, e1_recv, got, gu_send, gu_recv, far3, far4, passed, h_send, h_recv, s2_send, s2_recv,
    gath, pre, slot_rows, e2_send, e2_recv,
    e_sems, r_sems, s_sems, ready,
):
    ex = lax.axis_index("expert")
    dp = lax.axis_index("dp")
    z = dp // SIDE
    x = dp % SIDE
    even = ex % 2 == 0
    first = jnp.where(even, x, z)
    second = jnp.where(even, z, x)
    first_step = jnp.where(even, 1, SIDE)
    second_step = jnp.where(even, SIDE, 1)

    def along_first(k):
        to = (first + k) % SIDE
        return (ex, dp + (to - first) * first_step), to

    def along_second(k):
        to = (second + k) % SIDE
        return (ex, dp + (to - second) * second_step), to

    def along_expert(k):
        to = (ex + k) % PEERS
        return (to, dp), to

    barrier = pltpu.get_barrier_semaphore()

    def greet(who, count):
        @pl.loop(1, count)
        def _(k):
            pl.semaphore_signal(
                barrier, inc=1, device_id=who(k)[0], device_id_type=pl.DeviceIdType.MESH
            )

    loads = {
        "x": (x_hbm, x_ref), "w0": (w_hbm.at[0], w_ref.at[0]), "w1": (w_hbm.at[1], w_ref.at[1]),
        "w2": (w_hbm.at[2], w_ref.at[2]), "og": (og_hbm, og_ref), "rt": (rt_hbm, rt_ref),
        "gt": (gt_hbm, gt_ref), "d": (d_hbm, d_ref),
    }
    loads = {
        name: pltpu.make_async_copy(src, dst, in_sems.at[i])
        for i, (name, (src, dst)) in enumerate(loads.items())
    }
    for load in loads.values():
        load.start()
    def along_x(k):
        to = (x + k) % SIDE
        return (ex, z * SIDE + to), to

    def at_z(to):
        return (ex, to * SIDE + x)

    greet(along_expert, PEERS)
    greet(along_x, SIDE)

    @pl.loop(z + 1, SIDE)
    def _(to):
        pl.semaphore_signal(
            barrier, inc=1, device_id=at_z(to), device_id_type=pl.DeviceIdType.MESH
        )

    def await_ready(k, turn):
        to = (z + k) % SIDE

        @pl.when(jnp.logical_and(turn, to > z))
        def _():
            pl.semaphore_wait(ready.at[to], 1)

    def send(src, dst, send_sem, recv_sem, device):
        pltpu.make_async_remote_copy(
            src_ref=src, dst_ref=dst, send_sem=send_sem, recv_sem=recv_sem,
            device_id=device, device_id_type=pl.DeviceIdType.MESH,
        ).start()

    def wait(ref, sem):
        pltpu.make_async_copy(ref, ref, sem).wait()

    loads["x"].wait()
    for e in range(MINE):
        loads[f"w{e}"].wait()
        for n in range(2048 // TILE):
            part = jnp.dot(
                x_ref[e], w_ref[e, :, n * TILE : (n + 1) * TILE], preferred_element_type=F32
            ).astype(BF16)
            kind, at = divmod(n * TILE, 1024)
            for i in range(TILE // 128):
                gu_send[at // 128 + i, e, kind * SLOTS : (kind + 1) * SLOTS, :] = part[
                    :, i * 128 : (i + 1) * 128
                ]

    for name in ("og", "rt", "gt"):
        loads[name].wait()
    og_pad[...] = jnp.zeros_like(og_pad)
    og_pad[0:12, 0:112] = og_ref[...]
    rt_pad[...] = jnp.full_like(rt_pad, -2)
    rt_pad[:, 0:12] = rt_ref[...]
    gt_pad[...] = jnp.zeros_like(gt_pad)
    gt_pad[:, 0:12] = gt_ref[...]
    shape = (PEERS * 16, 128)
    row = lax.broadcasted_iota(jnp.int32, shape, 0)
    which = (row >> 2) & 3
    expert_id = jnp.where(which < MINE, (row >> 4) * MINE + which, -1)
    names = jnp.zeros(shape, F32)
    gate = jnp.zeros(shape, F32)
    for k in range(8):
        hit = rt_pad[k : k + 1, :] == expert_id
        names = names + jnp.where(hit, 1.0, 0.0)
        gate = gate + jnp.where(hit, gt_pad[k : k + 1, :], 0.0)
    before = lax.broadcasted_iota(jnp.int32, (128, 128), 0) < lax.broadcasted_iota(
        jnp.int32, (128, 128), 1
    )
    rank = jnp.dot(
        names.astype(BF16), jnp.where(before, 1.0, 0.0).astype(BF16), preferred_element_type=F32
    )
    fills = jnp.where(rank == (row & 3).astype(F32), names, 0.0)
    gate_of = jnp.sum(fills * gate, axis=1, keepdims=True)
    table[...] = fills.astype(BF16)
    rows_out = jnp.dot(table[...], og_pad[...], preferred_element_type=F32) * gate_of
    e1_send[...] = rows_out.astype(BF16).reshape(PEERS, 16, 128)

    pl.semaphore_wait(barrier, SIDE - 1 + PEERS - 1 + z)

    @pl.loop(0, z)
    def _(to):
        pl.semaphore_signal(
            ready.at[z], inc=1, device_id=at_z(to), device_id_type=pl.DeviceIdType.MESH
        )

    @pl.loop(1, PEERS)
    def _(k):
        device, to = along_expert(k)
        send(e1_send.at[to], e1_recv.at[ex], e_sems.at[0], e_sems.at[1], device)

    e1_recv[ex] = e1_send[ex]

    odd = jnp.logical_not(even)
    for side, way in ((1, 1), (0, -1)):
        one, next_one = along_first(way)
        two, _ = along_first(2 * way)
        _, third = along_first(3 * way)
        _, fourth = along_first(4)
        half = pl.ds(side * SLOTS, SLOTS)
        await_ready(way, odd)
        for e in range(MINE):
            send(gu_send.at[third, e], far3.at[e, side], s_sems.at[5, e], r_sems.at[5, e], one)
        await_ready(2 * way, odd)
        for e in range(MINE):
            send(
                gu_send.at[fourth, e, half], far4.at[e, side],
                s_sems.at[6, e], r_sems.at[6, e], two,
            )
        for e in range(MINE):
            send(gu_send.at[next_one, e], gu_recv.at[e, side], s_sems.at[0, e], r_sems.at[0, e], one)
    for e in range(MINE):
        wait(far3.at[e], r_sems.at[5, e])
        wait(far4.at[e], r_sems.at[6, e])
        for side, way in enumerate((-1, 1)):
            two, second_one = along_first(2 * way)
            total = gu_send[second_one, e].astype(F32) + far3[e, side].astype(F32)
            extra = far4[e, side].astype(F32)
            parts = [total[0:SLOTS], total[SLOTS:]]
            parts[side] = parts[side] + extra
            passed[e, side, 0:SLOTS] = parts[0].astype(BF16)
            passed[e, side, SLOTS:] = parts[1].astype(BF16)
            send(passed.at[e, side], gu_recv.at[e, 2 + side], s_sems.at[0, e], r_sems.at[0, e], two)

    loads["d"].wait()
    wait(e1_recv.at[0 : PEERS - 1], e_sems.at[1])
    take = lax.broadcasted_iota(jnp.int32, (MINE * SLOTS, 256), 0)
    lane = lax.broadcasted_iota(jnp.int32, (MINE * SLOTS, 256), 1)
    source = ((take >> 2) & 15) * 16 + (take >> 6) * 4 + (take & 3)
    pick = jnp.where(lane == source, 1.0, 0.0).astype(BF16)
    got[...] = jnp.dot(
        pick, e1_recv[...].reshape(PEERS * 16, 128), preferred_element_type=F32
    ).astype(BF16)
    for k in (3, 4, 5):
        await_ready(k, odd)
    for e in range(MINE):
        for n in range(1024 // TILE):
            part = jnp.dot(
                got[e * SLOTS : (e + 1) * SLOTS, 0:112],
                d_ref[e, :, n * TILE : (n + 1) * TILE],
                preferred_element_type=F32,
            ).astype(BF16)
            for i in range(TILE // 128):
                h_send[n * TILE // 128 + i, e] = part[:, i * 128 : (i + 1) * 128]

        @pl.loop(1, SIDE)
        def _(k):
            device, to = along_first(k)
            send(h_send.at[to, e], h_recv.at[e, k - 1], s_sems.at[1, e], r_sems.at[1, e], device)

    for k in range(1, SIDE):
        await_ready(k, even)
    for e in range(MINE):
        wait(gu_recv.at[e], r_sems.at[0, e])
        total = gu_send[first, e].astype(F32)
        for k in range(4):
            total = total + gu_recv[e, k].astype(F32)
        s2_send[:, e, 0:8, :] = total[0:SLOTS].reshape(SIDE, 8, 128)
        s2_send[:, e, 8:16, :] = total[SLOTS:].reshape(SIDE, 8, 128)
        wait(h_recv.at[e], r_sems.at[1, e])
        total = h_send[first, e].astype(F32)
        for k in range(SIDE - 1):
            total = total + h_recv[e, k].astype(F32)
        s2_send[:, e, 16:24, :] = total.reshape(SIDE, 8, 128)

        @pl.loop(1, SIDE)
        def _(k):
            device, to = along_second(k)
            send(s2_send.at[to, e], s2_recv.at[e, k - 1], s_sems.at[2, e], r_sems.at[2, e], device)

    for e in range(MINE):
        wait(s2_recv.at[e], r_sems.at[2, e])
        total = s2_send[second, e]
        for k in range(SIDE - 1):
            total = total + s2_recv[e, k]
        gate_pre, up_pre, hidden = total[0:8], total[8:16], total[16:24]
        sg = 1.0 / (1.0 + jnp.exp(-gate_pre))
        slope = sg * (1.0 + gate_pre * (1.0 - sg))
        both = jnp.concatenate([hidden * up_pre * slope, hidden * gate_pre * sg], axis=0)
        gath[e, first, second] = both.astype(BF16)

        @pl.loop(1, SIDE)
        def _(k):
            device, _to = along_second(k)
            here = gath.at[e, first, second]
            send(here, here, s_sems.at[3, e], r_sems.at[3, e], device)

    for e in range(MINE):
        wait(gath.at[e, 0, 0 : SIDE - 1], r_sems.at[3, e])

        @pl.loop(0, SIDE - 1)
        def _(k):
            skip = jnp.where(k >= z, k + 1, k) - z
            device, _to = along_first(jnp.where(even, k + 1, skip + SIDE))
            here = gath.at[e, first]
            send(here, here, s_sems.at[4, e], r_sems.at[4, e], device)

    slot_rows[...] = jnp.zeros_like(slot_rows)
    for e in range(MINE):
        wait(gath.at[e, 0 : SIDE - 1], r_sems.at[4, e])
        for j in range(SIDE):
            block = gath[e, j].astype(F32)
            pre[e, :, j * 128 : (j + 1) * 128] = block[:, 0:8].reshape(SLOTS, 128).astype(BF16)
            pre[e, :, 1024 + j * 128 : 1024 + (j + 1) * 128] = (
                block[:, 8:16].reshape(SLOTS, 128).astype(BF16)
            )
        slot_rows[e * SLOTS : (e + 1) * SLOTS, 0:112] = lax.dot_general(
            pre[e], w_ref[e], (((1,), (1,)), ((), ())), preferred_element_type=F32
        ).astype(BF16)
    back = lax.broadcasted_iota(jnp.int32, (256, 256), 0)
    lane = lax.broadcasted_iota(jnp.int32, (256, 256), 1)
    source = jnp.where(
        ((back >> 2) & 3) < MINE, ((back >> 2) & 3) * SLOTS + (back >> 4) * 4 + (back & 3), -1
    )
    e2_send[...] = (
        jnp.dot(
            jnp.where(lane == source, 1.0, 0.0).astype(BF16),
            slot_rows[...],
            preferred_element_type=F32,
        )
        .astype(BF16)
        .reshape(PEERS, 16, 128)
    )

    @pl.loop(1, PEERS)
    def _(k):
        device, to = along_expert(k)
        send(e2_send.at[to], e2_recv.at[ex], e_sems.at[2], e_sems.at[3], device)

    e2_recv[ex] = e2_send[ex]

    for e in range(MINE):
        for n in range(2048 // TILE):
            cols = slice(n * TILE, (n + 1) * TILE)
            wg_ref[e, :, cols] = lax.dot_general(
                x_ref[e], pre[e, :, cols], (((0,), (0,)), ((), ())), preferred_element_type=F32
            ).astype(BF16)

    wait(e2_recv.at[0 : PEERS - 1], e_sems.at[3])
    token = lax.dot_general(
        table[...],
        e2_recv[...].reshape(PEERS * 16, 128),
        (((0,), (0,)), ((), ())),
        preferred_element_type=F32,
    )
    ig_ref[...] = token[0:12, 0:112].astype(BF16)

    wait(e1_send.at[0 : PEERS - 1], e_sems.at[0])
    wait(e2_send.at[0 : PEERS - 1], e_sems.at[2])
    for e in range(MINE):
        wait(gu_recv.at[e], s_sems.at[0, e])
        wait(far3.at[e], s_sems.at[5, e])
        wait(far4.at[e], s_sems.at[6, e])
        wait(h_recv.at[e], s_sems.at[1, e])
        wait(s2_recv.at[e], s_sems.at[2, e])
        wait(gath.at[e, 0, 0 : SIDE - 1], s_sems.at[3, e])
        wait(gath.at[e, 0 : SIDE - 1], s_sems.at[4, e])


def body(output_grad, routing, gates, saved_inputs, gate_up, down_weight):
    dma = pltpu.SemaphoreType.DMA
    return pl.pallas_call(
        kernel,
        out_shape=(
            jax.ShapeDtypeStruct(output_grad.shape, BF16),
            jax.ShapeDtypeStruct(gate_up.shape, BF16),
        ),
        in_specs=[pl.BlockSpec(memory_space=pltpu.HBM)] * 6,
        out_specs=(pl.BlockSpec(memory_space=pltpu.VMEM),) * 2,
        scratch_shapes=[
            pltpu.VMEM((12, 112), BF16),
            pltpu.VMEM((8, 12), jnp.int32),
            pltpu.VMEM((8, 12), F32),
            pltpu.VMEM((MINE, SLOTS, 112), BF16),
            pltpu.VMEM((MINE, 112, 2048), BF16),
            pltpu.VMEM((MINE, 112, 1024), BF16),
            dma((8,)),
            pltpu.VMEM((128, 128), BF16),
            pltpu.VMEM((8, 128), jnp.int32),
            pltpu.VMEM((8, 128), F32),
            pltpu.VMEM((256, 128), BF16),
            pltpu.VMEM((PEERS, 16, 128), BF16),
            pltpu.VMEM((PEERS, 16, 128), BF16),
            pltpu.VMEM((MINE * SLOTS, 128), BF16),
            pltpu.VMEM((SIDE, MINE, 2 * SLOTS, 128), BF16),
            pltpu.VMEM((MINE, 4, 2 * SLOTS, 128), BF16),
            pltpu.VMEM((MINE, 2, 2 * SLOTS, 128), BF16),
            pltpu.VMEM((MINE, 2, SLOTS, 128), BF16),
            pltpu.VMEM((MINE, 2, 2 * SLOTS, 128), BF16),
            pltpu.VMEM((SIDE, MINE, SLOTS, 128), BF16),
            pltpu.VMEM((MINE, SIDE - 1, SLOTS, 128), BF16),
            pltpu.VMEM((SIDE, MINE, 24, 128), F32),
            pltpu.VMEM((MINE, SIDE - 1, 24, 128), F32),
            pltpu.VMEM((MINE, SIDE, SIDE, 16, 128), BF16),
            pltpu.VMEM((MINE, SLOTS, 2048), BF16),
            pltpu.VMEM((256, 128), BF16),
            pltpu.VMEM((PEERS, 16, 128), BF16),
            pltpu.VMEM((PEERS, 16, 128), BF16),
            dma((4,)),
            dma((7, MINE)),
            dma((7, MINE)),
            pltpu.SemaphoreType.REGULAR((SIDE,)),
        ],
        compiler_params=pltpu.CompilerParams(
            collective_id=1, has_side_effects=True, vmem_limit_bytes=24 << 20
        ),
    )(
        *(
            pltpu.with_memory_space_constraint(v, pltpu.HBM)
            for v in (
                output_grad, routing.T, gates.T, saved_inputs, gate_up,
                jnp.swapaxes(down_weight, 1, 2),
            )
        )
    )


def solution(mesh):
    placed = (
        P("expert", "dp"),
        P("expert", None),
        P("expert", None),
        P("expert", None, "dp"),
        P("expert", "dp", None),
        P("expert", None, "dp"),
    )
    return jax.shard_map(
        body,
        mesh=mesh,
        in_specs=placed,
        out_specs=(P("expert", "dp"), P("expert", "dp", None)),
        check_vma=False,
    )
```
